512 devices in a mesh: fsdp: 32 (over z, core), tp: 16 (over y, x).
Axes of the slice: x: 4, y: 4, z: 16, core: 2. Of those that a mesh axis runs over, the one named last changes fastest.
Arguments:
- momentum: bfloat16 [8192, 28672], P('fsdp', 'tp'), may hold values from -256 to 256
- gradient: bfloat16 [8192, 28672], P('fsdp', 'tp'), may hold values from -256 to 256
- weight: bfloat16 [8192, 28672], P('fsdp', 'tp'), may hold values from -0.75 to 0.75
- right_factor: bfloat16 [512, 28672], P('fsdp', 'tp'), may hold values from -6 to 6
Outputs:
- new_momentum: bfloat16 [8192, 28672], P('fsdp', 'tp')
- new_weight: bfloat16 [8192, 28672], P('fsdp', 'tp')
- new_factor: bfloat16 [512, 28672], P('fsdp', 'tp')
The draws below stay inside these ranges and needn't reach their ends.
All inputs are finite; a program needn't handle non-finite values.
Results may differ from the reference program's by a relative error of at most 0.013.
Values may be sent and summed in bfloat16 or wider, within the bound.
No kernel may reach another device: no remote copies, remote signals or barrier semaphores. Data moves between devices by JAX's collectives and lax.ppermute only.
A program may use at most 64 MiB of HBM per device.

```python
import jax
import jax.numpy as jnp
from jax import lax

DM = 8192
DF = 28672
RANK = 512


def scale_grid(key):
    row_key, col_key = jax.random.split(key)
    row_part = jnp.exp(jax.random.uniform(row_key, (DM,), jnp.float32, jnp.log(0.4), jnp.log(1.3)))
    row_part = row_part * 10.0 ** (jnp.arange(DM, dtype=jnp.float32) / DM)
    col_part = jnp.exp(jax.random.uniform(col_key, (DF,), jnp.float32, jnp.log(0.4), jnp.log(1.3)))
    col_part = col_part * 3.0 ** (jnp.arange(DF, dtype=jnp.float32) / DF)
    return row_part[:, None] * col_part[None, :]


def draw_momentum(key, part):
    scales = scale_grid(key)
    key = jax.random.fold_in(key, 11)
    values = jnp.clip(jax.random.normal(key, (DM, DF), jnp.float32), -5.0, 5.0)
    return (values * scales).astype(jnp.bfloat16)


def draw_gradient(key, part):
    scales = scale_grid(key)
    key = jax.random.fold_in(key, 12)
    values = jnp.clip(jax.random.normal(key, (DM, DF), jnp.float32), -5.0, 5.0)
    return (values * scales).astype(jnp.bfloat16)


def block_levels(rng, dims, cuts, low, top_value):
    factor_of = 1.0
    for position, shards_of in cuts:
        heights = jax.random.uniform(jax.random.fold_in(jax.random.fold_in(rng, 6), position), (shards_of,), jnp.float32, low / len(cuts), top_value / len(cuts))
        factor_of = factor_of * jnp.repeat(jnp.exp(heights), dims[position] // shards_of).reshape((-1,) + (1,) * (len(dims) - 1 - position))
    return factor_of


def noise(rng, dims, spread, reach, cuts=(), kind=jnp.bfloat16):
    array = jax.random.normal(rng, dims, jnp.float32) * spread
    if len(cuts) > 0:
        array = block_levels(rng, dims, cuts, -0.22, 0.18) * array
    return jnp.clip(array, min=-reach, max=reach).astype(kind)


def setup_inputs(seed: int = 0) -> dict:
    arg_keys = jax.random.split(jax.random.key(seed), 5)
    momentum = draw_momentum(jax.random.fold_in(arg_keys[4], 71), 0)
    gradient = draw_gradient(jax.random.fold_in(arg_keys[4], 71), 0)
    weight = noise(arg_keys[2], (DM, DF), 0.05, 0.75, ((0, 32), (1, 16)))
    right_factor = noise(arg_keys[3], (RANK, DF), 1.0, 6.0, ((0, 32), (1, 16)))
    return dict(momentum=momentum, gradient=gradient, weight=weight, right_factor=right_factor)


def reference(momentum, gradient, weight, right_factor):
    blend = (momentum.astype(jnp.float32) + gradient.astype(jnp.float32)).astype(jnp.bfloat16)
    start = jnp.dot(blend.astype(jnp.float32), right_factor.T.astype(jnp.float32), preferred_element_type=jnp.float32)
    gram = jnp.dot(start.T, start, precision=lax.Precision.HIGHEST)
    lower = jnp.linalg.cholesky(gram)
    basis = jax.scipy.linalg.solve_triangular(lower, start.T, lower=True).T.astype(jnp.bfloat16)
    project = jnp.dot(basis.T.astype(jnp.float32), blend.astype(jnp.float32), preferred_element_type=jnp.float32).astype(jnp.bfloat16)
    wide = project.astype(jnp.float32)
    rms = jnp.sqrt(lax.optimization_barrier(jnp.mean(wide * wide, axis=1, keepdims=True)) + 1e-06)
    new_factor = (wide / rms).astype(jnp.bfloat16)
    feedback = jnp.dot(basis.astype(jnp.float32), project.astype(jnp.float32), preferred_element_type=jnp.float32)
    new_momentum = (blend.astype(jnp.float32) - 0.4 * feedback).astype(jnp.bfloat16)
    update = jnp.dot(basis.astype(jnp.float32), new_factor.astype(jnp.float32), preferred_element_type=jnp.float32)
    new_weight = (weight.astype(jnp.float32) - 2.0 * jnp.sqrt(DM / DF) * update).astype(jnp.bfloat16)
    return (new_momentum, new_weight, new_factor)
```

```python
import math

import jax
import jax.numpy as jnp
from jax import lax
from jax.sharding import PartitionSpec as P

DM = 8192
DF = 28672
Z, Y, X = 16, 4, 4
HI = lax.Precision.HIGHEST
F32 = jnp.float32
BF16 = jnp.bfloat16


def from_z(value, step):
    perm = [(((z + step) % Z) * 2 + c, z * 2 + c) for z in range(Z) for c in range(2)]
    return lax.ppermute(value, "fsdp", perm)


def from_core(value):
    return lax.ppermute(value, "fsdp", [(i ^ 1, i) for i in range(2 * Z)])


def from_x(value, step):
    perm = [(y * X + (x + step) % X, y * X + x) for y in range(Y) for x in range(X)]
    return lax.ppermute(value, "tp", perm)


def from_y(value, step):
    perm = [(((y + step) % Y) * X + x, y * X + x) for y in range(Y) for x in range(X)]
    return lax.ppermute(value, "tp", perm)


def ordered(pieces, first):
    rows = []
    for place in range(4):
        row = pieces[place]
        for start in range(1, 4):
            row = jnp.where(first == start, pieces[(place - start) % 4], row)
        rows.append(row)
    return jnp.stack(rows)


def gather_fsdp(chunk, core, quad, lane):
    far = ordered([chunk] + [from_z(chunk, 4 * j) for j in (1, 2, 3)], quad)
    ahead, behind = from_z(far, 1), from_z(far, -1)
    across = jnp.concatenate([from_z(far[:2], 2), from_z(far[2:], -2)])
    near = ordered([far, ahead, across, behind], lane)
    other = from_core(near)
    return jnp.stack([jnp.where(core == 0, near, other), jnp.where(core == 0, other, near)])


def scatter_fsdp(total, core, quad, lane):
    pick = lambda array, place: lax.dynamic_index_in_dim(array, place, 0, keepdims=False)
    half = pick(total, core) + from_core(pick(total, 1 - core))
    ahead = from_z(pick(half, (lane + 3) % 4), 1)
    behind = from_z(pick(half, (lane + 1) % 4), -1)
    across = pick(half, (lane + 2) % 4)
    across = jnp.concatenate([from_z(across[:2], 2), from_z(across[2:], -2)])
    mine = pick(half, lane) + ahead + behind + across
    out = pick(mine, quad)
    for j in (1, 2, 3):
        out = out + from_z(pick(mine, (quad - j) % 4), 4 * j)
    return out


def sum_tp(value):
    value = value + from_x(value, 1) + from_x(value, 2) + from_x(value, 3)
    return value + from_y(value, 1) + from_y(value, 2) + from_y(value, 3)


def gather_tp(chunk, row, col):
    line = ordered([chunk] + [from_x(chunk, j) for j in (1, 2, 3)], col)
    return ordered([line] + [from_y(line, j) for j in (1, 2, 3)], row)


def inverse_factor(gram):
    lower = jnp.linalg.cholesky(gram)
    return jax.scipy.linalg.solve_triangular(lower, jnp.eye(512, dtype=F32), lower=True)


def nt(a, b, precision=None):
    return lax.dot_general(
        a, b, (((1,), (1,)), ((), ())), precision=precision, preferred_element_type=F32
    )


def local(momentum, gradient, weight, right_factor):
    fsdp, tp = lax.axis_index("fsdp"), lax.axis_index("tp")
    core, z = fsdp % 2, fsdp // 2
    quad, lane = z // 4, z % 4
    row, col = tp // X, tp % X

    blend = (momentum.astype(F32) + gradient.astype(F32)).astype(BF16)

    factor = gather_fsdp(right_factor, core, quad, lane)
    factor = jnp.transpose(factor, (2, 1, 0, 3, 4)).reshape(512, -1)
    partial = nt(blend, factor)
    pieces = lax.all_to_all(partial.reshape(16, 16, 512), "tp", 0, 0)
    start = gather_tp(jnp.sum(pieces, axis=0), row, col).reshape(256, 512)

    gram = jnp.dot(start.T, start, precision=HI)
    band = lax.dynamic_index_in_dim(gram.reshape(16, 2, 16, 512), tp, 0, keepdims=False)
    pick = lambda place: lax.dynamic_index_in_dim(band, place, 0, keepdims=False)
    band = pick(core) + from_core(pick(1 - core))
    band = band + from_z(band, 1) + from_z(band, -1) + from_z(band, 2)
    band = band + from_z(band, 4) + from_z(band, -4) + from_z(band, 8)
    mine = gather_tp(band, row, col)
    other = from_core(mine)
    gram = jnp.stack(
        [jnp.where(core == 0, mine, other), jnp.where(core == 0, other, mine)], axis=2
    ).reshape(512, 512)

    high = start.astype(BF16)
    low = (start - high.astype(F32)).astype(BF16)
    tn = lambda a, b: lax.dot_general(
        a, b, (((0,), (0,)), ((), ())), preferred_element_type=F32
    )
    cross = (tn(blend, high) + tn(blend, low)).reshape(2, 4, 4, 56, 512)
    cross = scatter_fsdp(cross, core, quad, lane)

    inverse = inverse_factor(gram)
    chunk = nt(cross, inverse, HI).astype(BF16)
    project = gather_fsdp(chunk, core, quad, lane).reshape(1792, 512)
    basis = nt(start, inverse, HI).astype(BF16)

    wide = project.astype(F32)
    squares = sum_tp(jnp.sum(wide * wide, axis=0, keepdims=True))
    rms = jnp.sqrt(squares / DF + 1e-06)
    factor_t = (wide / rms).astype(BF16)
    chosen = (jnp.arange(512)[None, :] == 16 * fsdp + jnp.arange(16)[:, None]).astype(BF16)
    new_factor = nt(chosen, factor_t).astype(BF16)
    new_momentum = (blend.astype(F32) - 0.4 * nt(basis, project)).astype(BF16)
    new_weight = (
        weight.astype(F32) - 2.0 * math.sqrt(DM / DF) * nt(basis, factor_t)
    ).astype(BF16)
    return (new_momentum, new_weight, new_factor)


def solution(mesh):
    placed = (P("fsdp", "tp"), P("fsdp", "tp"), P("fsdp", "tp"), P("fsdp", "tp"))
    return jax.shard_map(
        local,
        mesh=mesh,
        in_specs=placed,
        out_specs=(P("fsdp", "tp"), P("fsdp", "tp"), P("fsdp", "tp")),
        check_vma=False,
    )
```

```python
import math

import jax
import jax.numpy as jnp
from jax import lax
from jax.experimental import pallas as pl
from jax.experimental.pallas import tpu as pltpu
from jax.sharding import PartitionSpec as P

DM = 8192
DF = 28672
Z = 16
HI = lax.Precision.HIGHEST
F32 = jnp.float32
BF16 = jnp.bfloat16
B = 128

LINE = [[(4 * q + k) * 2 + c for k in range(4) for q in range(4)] for c in range(2)]
DEEP = [[z * 2 + c for z in range(Z)] for c in range(2)]
FAR = [[(4 * q + k) * 2 + c for q in range(4)] for k in range(4) for c in range(2)]
NEAR = [[(4 * q + k) * 2 + c for k in range(4)] for q in range(4) for c in range(2)]


def from_core(value):
    return lax.ppermute(value, "fsdp", [(i ^ 1, i) for i in range(2 * Z)])


def spread(value, axis, groups, size):
    return lax.all_to_all(
        jnp.broadcast_to(value, (size,) + value.shape), axis, 0, 0, axis_index_groups=groups
    )


def by_core(core, mine, other, axis):
    return jnp.stack(
        [jnp.where(core == 0, mine, other), jnp.where(core == 0, other, mine)], axis=axis
    )


def pick(array, place):
    return lax.dynamic_index_in_dim(array, place, 0, keepdims=False)


def factor_block(diag):
    sub = lax.broadcasted_iota(jnp.int32, (8, B), 0)
    lanes = lax.broadcasted_iota(jnp.int32, (8, B), 1)
    left = [diag[8 * i : 8 * i + 8] for i in range(B // 8)]
    right = [(lanes == sub + 8 * i).astype(F32) for i in range(B // 8)]
    done = []
    for p in range(B // 8):
        w, v = left[p], right[p]
        spread = lambda x, q: jnp.broadcast_to(x[:, 8 * p + q : 8 * p + q + 1], (8, B))
        full = lambda x, j: jnp.broadcast_to(x[j : j + 1], (8, B))
        cols = [spread(w, q) for q in range(8)]
        roots, above = [], {}
        for j in range(8):
            pivot = full(cols[j], j)
            root = lax.rsqrt(pivot)
            root = root * (1.5 - 0.5 * pivot * root * root)
            roots.append(root)
            col = jnp.where(sub > j, cols[j] * root, 0.0)
            for q in range(j + 1, 8):
                above[j, q] = full(cols[q], j) * root
                cols[q] = cols[q] - col * above[j, q]
            row = full(w, j) * root
            w = jnp.where(sub == j, row, w - col * row)
            row = full(v, j) * root
            v = jnp.where(sub == j, row, v - col * row)
        done.append(v)
        for i in range(p + 1, B // 8):
            a, e = left[i], right[i]
            cols = [spread(a, q) for q in range(8)]
            for j in range(8):
                col = cols[j] * roots[j]
                for q in range(j + 1, 8):
                    cols[q] = cols[q] - col * above[j, q]
                a = a - col * w[j : j + 1]
                e = e - col * v[j : j + 1]
            left[i], right[i] = a, e
    return jnp.concatenate(done)


def inverse_kernel(gram_ref, out_ref, work):
    work[...] = gram_ref[...]
    r = lax.broadcasted_iota(jnp.int32, (512, 512), 0)
    c = lax.broadcasted_iota(jnp.int32, (512, 512), 1)
    out_ref[...] = (r == c).astype(F32)

    @pl.loop(0, 4)
    def _(b):
        at = pl.multiple_of(b * B, B)
        rows = pl.ds(at, B)
        inv = factor_block(work[rows, pl.ds(at, B)])
        upper = jnp.dot(inv, work[rows, :], precision=HI, preferred_element_type=F32)
        lower = jnp.dot(inv, out_ref[rows, :], precision=HI, preferred_element_type=F32)
        out_ref[rows, :] = lower

        @pl.when(b < 3)
        def _():
            lane = lax.broadcasted_iota(jnp.int32, (B, 512), 1)
            coef = jnp.where(lane >= at + B, upper, 0.0)
            tn = lambda x, y: lax.dot_general(
                x, y, (((0,), (0,)), ((), ())), precision=HI, preferred_element_type=F32
            )
            work[...] = work[...] - tn(coef, upper)
            out_ref[...] = out_ref[...] - tn(coef, lower)


def inverse_factor(gram):
    return pl.pallas_call(
        inverse_kernel,
        out_shape=jax.ShapeDtypeStruct((512, 512), F32),
        in_specs=[pl.BlockSpec(memory_space=pltpu.VMEM)],
        out_specs=pl.BlockSpec(memory_space=pltpu.VMEM),
        scratch_shapes=[pltpu.VMEM((512, 512), F32)],
        compiler_params=pltpu.CompilerParams(vmem_limit_bytes=24 * 1024 * 1024),
        cost_estimate=pl.CostEstimate(flops=6 * 10**8, bytes_accessed=3 * 2**20, transcendentals=512),
        name="inverse_factor",
    )(gram)


def nt(a, b, precision=None):
    return lax.dot_general(
        a, b, (((1,), (1,)), ((), ())), precision=precision, preferred_element_type=F32
    )


def tn(a, b):
    return lax.dot_general(a, b, (((0,), (0,)), ((), ())), preferred_element_type=F32)


def local(momentum, gradient, weight, right_factor):
    fsdp, tp = lax.axis_index("fsdp"), lax.axis_index("tp")
    core = fsdp % 2

    blend = (momentum.astype(F32) + gradient.astype(F32)).astype(BF16)

    mine = lax.all_gather(right_factor, "fsdp", axis_index_groups=DEEP)
    factor = by_core(core, mine, from_core(mine), 1).reshape(512, -1)
    partial = nt(blend, factor)
    pieces = lax.all_to_all(partial.reshape(16, 16, 512), "tp", 0, 0)
    start = spread(jnp.sum(pieces, axis=0), "tp", None, 16).reshape(256, 512)

    high = start.astype(BF16)
    low = (start - high.astype(F32)).astype(BF16)
    cross = (tn(blend, high) + tn(blend, low)).reshape(2, 16, 56, 512)
    cross = pick(cross, core) + from_core(pick(cross, 1 - core))
    cross = lax.psum_scatter(cross, "fsdp", scatter_dimension=0, axis_index_groups=LINE)

    gram = jnp.dot(start.T, start, precision=HI)
    band = pick(gram.reshape(16, 2, 16, 512), tp)
    band = pick(band, core) + from_core(pick(band, 1 - core))
    band = jnp.sum(spread(band, "fsdp", NEAR, 4), axis=0)
    band = jnp.sum(spread(band, "fsdp", FAR, 4), axis=0)
    mine = spread(band, "tp", None, 16)
    gram = by_core(core, mine, from_core(mine), 1).reshape(512, 512)

    inverse = inverse_factor(gram)
    chunk = nt(cross, inverse, HI).astype(BF16)
    mine = spread(spread(chunk, "fsdp", FAR, 4), "fsdp", NEAR, 4)
    project = by_core(core, mine, from_core(mine), 0).reshape(1792, 512)
    basis = nt(start, inverse, HI).astype(BF16)

    wide = project.astype(F32)
    squares = jnp.sum(wide * wide, axis=0, keepdims=True)
    squares = jnp.sum(spread(squares, "tp", None, 16), axis=0)
    rms = jnp.sqrt(squares / DF + 1e-06)
    factor_t = (wide / rms).astype(BF16)
    chosen = (jnp.arange(512)[None, :] == 16 * fsdp + jnp.arange(16)[:, None]).astype(BF16)
    new_factor = nt(chosen, factor_t).astype(BF16)
    new_momentum = (blend.astype(F32) - 0.4 * nt(basis, project)).astype(BF16)
    new_weight = (
        weight.astype(F32) - 2.0 * math.sqrt(DM / DF) * nt(basis, factor_t)
    ).astype(BF16)
    return (new_momentum, new_weight, new_factor)


def solution(mesh):
    placed = (P("fsdp", "tp"), P("fsdp", "tp"), P("fsdp", "tp"), P("fsdp", "tp"))
    return jax.shard_map(
        local,
        mesh=mesh,
        in_specs=placed,
        out_specs=(P("fsdp", "tp"), P("fsdp", "tp"), P("fsdp", "tp")),
        check_vma=False,
    )
```

```python
import math

import jax
import jax.numpy as jnp
from jax import lax
from jax.experimental import pallas as pl
from jax.experimental.pallas import tpu as pltpu
from jax.sharding import PartitionSpec as P

DM = 8192
DF = 28672
Z = 16
HI = lax.Precision.HIGHEST
F32 = jnp.float32
BF16 = jnp.bfloat16
B = 128

DEEP = [[z * 2 + c for z in range(Z)] for c in range(2)]


def from_core(value):
    return lax.ppermute(value, "fsdp", [(i ^ 1, i) for i in range(2 * Z)])


def spread(value, axis, groups, size):
    return lax.all_to_all(
        jnp.broadcast_to(value, (size,) + value.shape), axis, 0, 0, axis_index_groups=groups
    )


def by_core(core, mine, other, axis):
    return jnp.stack(
        [jnp.where(core == 0, mine, other), jnp.where(core == 0, other, mine)], axis=axis
    )


def pick(array, place):
    return lax.dynamic_index_in_dim(array, place, 0, keepdims=False)


def factor_block(diag):
    sub = lax.broadcasted_iota(jnp.int32, (8, B), 0)
    lanes = lax.broadcasted_iota(jnp.int32, (8, B), 1)
    left = [diag[8 * i : 8 * i + 8] for i in range(B // 8)]
    right = [(lanes == sub + 8 * i).astype(F32) for i in range(B // 8)]
    done = []
    for p in range(B // 8):
        w, v = left[p], right[p]
        spread = lambda x, q: jnp.broadcast_to(x[:, 8 * p + q : 8 * p + q + 1], (8, B))
        full = lambda x, j: jnp.broadcast_to(x[j : j + 1], (8, B))
        cols = [spread(w, q) for q in range(8)]
        roots, above = [], {}
        for j in range(8):
            pivot = full(cols[j], j)
            root, inv = lax.rsqrt(pivot), pl.reciprocal(pivot, approx=True)
            roots.append(root)
            for q in range(j + 1, 8):
                across = full(cols[q], j)
                above[j, q] = across * root
                cols[q] = cols[q] - (cols[j] * across) * inv
            col = jnp.where(sub > j, cols[j] * root, 0.0)
            row = full(w, j) * root
            w = jnp.where(sub == j, row, w - col * row)
            row = full(v, j) * root
            v = jnp.where(sub == j, row, v - col * row)
        done.append(v)
        for i in range(p + 1, B // 8):
            a, e = left[i], right[i]
            cols = [spread(a, q) for q in range(8)]
            for j in range(8):
                col = cols[j] * roots[j]
                for q in range(j + 1, 8):
                    cols[q] = cols[q] - col * above[j, q]
                a = a - col * w[j : j + 1]
                e = e - col * v[j : j + 1]
            left[i], right[i] = a, e
    return jnp.concatenate(done)


def inverse_kernel(gram_ref, out_ref, work):
    work[...] = gram_ref[...]
    r = lax.broadcasted_iota(jnp.int32, (512, 512), 0)
    c = lax.broadcasted_iota(jnp.int32, (512, 512), 1)
    out_ref[...] = (r == c).astype(F32)

    @pl.loop(0, 4)
    def _(b):
        at = pl.multiple_of(b * B, B)
        rows = pl.ds(at, B)
        inv = factor_block(work[rows, pl.ds(at, B)])
        upper = jnp.dot(inv, work[rows, :], precision=HI, preferred_element_type=F32)
        lower = jnp.dot(inv, out_ref[rows, :], precision=HI, preferred_element_type=F32)
        out_ref[rows, :] = lower

        @pl.when(b < 3)
        def _():
            lane = lax.broadcasted_iota(jnp.int32, (B, 512), 1)
            coef = jnp.where(lane >= at + B, upper, 0.0)
            tn = lambda x, y: lax.dot_general(
                x, y, (((0,), (0,)), ((), ())), precision=HI, preferred_element_type=F32
            )
            work[...] = work[...] - tn(coef, upper)
            out_ref[...] = out_ref[...] - tn(coef, lower)


def inverse_factor(gram):
    return pl.pallas_call(
        inverse_kernel,
        out_shape=jax.ShapeDtypeStruct((512, 512), F32),
        in_specs=[pl.BlockSpec(memory_space=pltpu.VMEM)],
        out_specs=pl.BlockSpec(memory_space=pltpu.VMEM),
        scratch_shapes=[pltpu.VMEM((512, 512), F32)],
        compiler_params=pltpu.CompilerParams(vmem_limit_bytes=24 * 1024 * 1024),
        cost_estimate=pl.CostEstimate(flops=6 * 10**8, bytes_accessed=3 * 2**20, transcendentals=512),
        name="inverse_factor",
    )(gram)


def nt(a, b, precision=None):
    return lax.dot_general(
        a, b, (((1,), (1,)), ((), ())), precision=precision, preferred_element_type=F32
    )


def tn(a, b):
    return lax.dot_general(a, b, (((0,), (0,)), ((), ())), preferred_element_type=F32)


def local(momentum, gradient, weight, right_factor):
    fsdp, tp = lax.axis_index("fsdp"), lax.axis_index("tp")
    core = fsdp % 2

    blend = (momentum.astype(F32) + gradient.astype(F32)).astype(BF16)

    half = blend.shape[1] // 2
    columns = lambda place: lax.dynamic_slice_in_dim(blend, place * half, half, axis=1)
    mine, other = columns(core), from_core(columns(1 - core))

    rows = lax.all_gather(right_factor, "fsdp", axis_index_groups=DEEP)
    factor = by_core(core, rows, from_core(rows), 1).reshape(512, -1)
    partial = nt(blend, factor)
    pieces = lax.all_to_all(partial.reshape(16, 16, 512), "tp", 0, 0)
    start = spread(jnp.sum(pieces, axis=0), "tp", None, 16).reshape(256, 512)
    second = from_core(start)

    def parts(array):
        high = array.astype(BF16)
        return high, (array - high.astype(F32)).astype(BF16)

    cross = sum(tn(mine, part) for part in parts(start))
    cross = cross + sum(tn(other, part) for part in parts(second))
    cross = lax.psum_scatter(
        cross.reshape(16, 56, 512), "fsdp", scatter_dimension=0, axis_index_groups=DEEP
    )

    gram = jnp.dot(start.T, start, precision=HI) + jnp.dot(second.T, second, precision=HI)
    band = pick(gram.reshape(32, 16, 512), 2 * tp + core)
    band = jnp.sum(lax.all_gather(band, "fsdp", axis_index_groups=DEEP), axis=0)
    bands = spread(band, "tp", None, 16)
    gram = by_core(core, bands, from_core(bands), 1).reshape(512, 512)

    inverse = inverse_factor(gram)
    chunk = nt(cross, inverse, HI).astype(BF16)
    rows = lax.all_gather(chunk, "fsdp", axis_index_groups=DEEP)
    project = by_core(core, rows, from_core(rows), 0).reshape(1792, 512)
    basis = nt(start, inverse, HI).astype(BF16)

    wide = project.astype(F32)
    squares = jnp.sum(wide * wide, axis=0, keepdims=True)
    squares = jnp.sum(spread(squares, "tp", None, 16), axis=0)
    rms = jnp.sqrt(squares / DF + 1e-06)
    factor_t = (wide / rms).astype(BF16)
    chosen = (jnp.arange(512)[None, :] == 16 * fsdp + jnp.arange(16)[:, None]).astype(BF16)
    new_factor = nt(chosen, factor_t).astype(BF16)
    new_momentum = (blend.astype(F32) - 0.4 * nt(basis, project)).astype(BF16)
    new_weight = (
        weight.astype(F32) - 2.0 * math.sqrt(DM / DF) * nt(basis, factor_t)
    ).astype(BF16)
    return (new_momentum, new_weight, new_factor)


def solution(mesh):
    placed = (P("fsdp", "tp"), P("fsdp", "tp"), P("fsdp", "tp"), P("fsdp", "tp"))
    return jax.shard_map(
        local,
        mesh=mesh,
        in_specs=placed,
        out_specs=(P("fsdp", "tp"), P("fsdp", "tp"), P("fsdp", "tp")),
        check_vma=False,
    )
```

```python
import math

import jax
import jax.numpy as jnp
from jax import lax
from jax.experimental import pallas as pl
from jax.experimental.pallas import tpu as pltpu
from jax.sharding import PartitionSpec as P

DM = 8192
DF = 28672
Z = 16
HI = lax.Precision.HIGHEST
F32 = jnp.float32
BF16 = jnp.bfloat16
B = 128

DEEP = [[z * 2 + c for z in range(Z)] for c in range(2)]
FAR = [[(4 * q + k) * 2 + c for q in range(4)] for k in range(4) for c in range(2)]
NEAR = [[(4 * q + k) * 2 + c for k in range(4)] for q in range(4) for c in range(2)]


def from_core(value):
    return lax.ppermute(value, "fsdp", [(i ^ 1, i) for i in range(2 * Z)])


def spread(value, axis, groups, size):
    return lax.all_to_all(
        jnp.broadcast_to(value, (size,) + value.shape), axis, 0, 0, axis_index_groups=groups
    )


def gather(value, groups):
    return lax.all_gather(value, "fsdp", axis_index_groups=groups)


def by_core(core, mine, other, axis):
    return jnp.stack(
        [jnp.where(core == 0, mine, other), jnp.where(core == 0, other, mine)], axis=axis
    )


def pick(array, place):
    return lax.dynamic_index_in_dim(array, place, 0, keepdims=False)


def factor_block(diag):
    sub = lax.broadcasted_iota(jnp.int32, (8, B), 0)
    lanes = lax.broadcasted_iota(jnp.int32, (8, B), 1)
    left = [diag[8 * i : 8 * i + 8] for i in range(B // 8)]
    right = [(lanes == sub + 8 * i).astype(F32) for i in range(B // 8)]
    done = []
    for p in range(B // 8):
        w, v = left[p], right[p]
        spread = lambda x, q: jnp.broadcast_to(x[:, 8 * p + q : 8 * p + q + 1], (8, B))
        full = lambda x, j: jnp.broadcast_to(x[j : j + 1], (8, B))
        cols = [spread(w, q) for q in range(8)]
        roots, above = [], {}
        for j in range(8):
            pivot = full(cols[j], j)
            root, inv = lax.rsqrt(pivot), pl.reciprocal(pivot, approx=True)
            roots.append(root)
            for q in range(j + 1, 8):
                across = full(cols[q], j)
                above[j, q] = across * root
                cols[q] = cols[q] - (cols[j] * across) * inv
            col = jnp.where(sub > j, cols[j] * root, 0.0)
            row = full(w, j) * root
            w = jnp.where(sub == j, row, w - col * row)
            row = full(v, j) * root
            v = jnp.where(sub == j, row, v - col * row)
        done.append(v)
        for i in range(p + 1, B // 8):
            a, e = left[i], right[i]
            cols = [spread(a, q) for q in range(8)]
            for j in range(8):
                col = cols[j] * roots[j]
                for q in range(j + 1, 8):
                    cols[q] = cols[q] - col * above[j, q]
                a = a - col * w[j : j + 1]
                e = e - col * v[j : j + 1]
            left[i], right[i] = a, e
    return jnp.concatenate(done)


def inverse_kernel(gram_ref, out_ref, work):
    work[...] = gram_ref[...]
    out_ref[...] = jnp.zeros_like(out_ref)

    def dot(x, y, axis):
        return lax.dot_general(
            x, y, (((axis,), (0,)), ((), ())), precision=HI, preferred_element_type=F32
        )

    @pl.loop(0, 4)
    def _(b):
        at = pl.multiple_of(b * B, B)
        inv = factor_block(work[pl.ds(at, B), pl.ds(at, B)])

        for i in range(4):

            @pl.when(b == i)
            def _():
                here, rest, before = (
                    slice(i * B, i * B + B), slice(i * B + B, 512), slice(0, i * B)
                )
                out_ref[here, here] = inv
                if i > 0:
                    lower = dot(inv, out_ref[here, before], 1)
                    out_ref[here, before] = lower
                if i < 3:
                    upper = dot(inv, work[here, rest], 1)
                    work[rest, rest] = work[rest, rest] - dot(upper, upper, 0)
                    out_ref[rest, here] = -dot(upper, inv, 0)
                    if i > 0:
                        out_ref[rest, before] = out_ref[rest, before] - dot(upper, lower, 0)


def inverse_factor(gram):
    return pl.pallas_call(
        inverse_kernel,
        out_shape=jax.ShapeDtypeStruct((512, 512), F32),
        in_specs=[pl.BlockSpec(memory_space=pltpu.VMEM)],
        out_specs=pl.BlockSpec(memory_space=pltpu.VMEM),
        scratch_shapes=[pltpu.VMEM((512, 512), F32)],
        compiler_params=pltpu.CompilerParams(vmem_limit_bytes=24 * 1024 * 1024),
        cost_estimate=pl.CostEstimate(flops=6 * 10**8, bytes_accessed=3 * 2**20, transcendentals=512),
        name="inverse_factor",
    )(gram)


def nt(a, b, precision=None):
    return lax.dot_general(
        a, b, (((1,), (1,)), ((), ())), precision=precision, preferred_element_type=F32
    )


def tn(a, b):
    return lax.dot_general(a, b, (((0,), (0,)), ((), ())), preferred_element_type=F32)


def local(momentum, gradient, weight, right_factor):
    fsdp, tp = lax.axis_index("fsdp"), lax.axis_index("tp")
    core = fsdp % 2

    blend = (momentum.astype(F32) + gradient.astype(F32)).astype(BF16)

    half = blend.shape[1] // 2
    columns = lambda place: lax.dynamic_slice_in_dim(blend, place * half, half, axis=1)
    mine, other = columns(core), from_core(columns(1 - core))

    rows = gather(gather(right_factor, FAR), NEAR)
    factor = by_core(core, rows, from_core(rows), 2)
    factor = jnp.swapaxes(factor, 0, 1).reshape(512, -1)
    partial = nt(blend, factor)
    pieces = lax.all_to_all(partial.reshape(16, 16, 512), "tp", 0, 0)
    start = spread(jnp.sum(pieces, axis=0), "tp", None, 16).reshape(256, 512)
    second = from_core(start)

    def parts(array):
        high = array.astype(BF16)
        return high, (array - high.astype(F32)).astype(BF16)

    cross = sum(tn(mine, part) for part in parts(start))
    cross = cross + sum(tn(other, part) for part in parts(second))
    cross = lax.psum_scatter(
        cross.reshape(16, 56, 512), "fsdp", scatter_dimension=0, axis_index_groups=DEEP
    )

    gram = jnp.dot(start.T, start, precision=HI) + jnp.dot(second.T, second, precision=HI)
    band = pick(gram.reshape(32, 16, 512), 2 * tp + core)
    band = jnp.sum(gather(jnp.sum(gather(band, NEAR), axis=0), FAR), axis=0)
    bands = spread(band, "tp", None, 16)
    gram = by_core(core, bands, from_core(bands), 1).reshape(512, 512)

    inverse = inverse_factor(gram)
    chunk = nt(cross, inverse, HI).astype(BF16)
    rows = gather(gather(chunk, FAR), NEAR)
    project = by_core(core, rows, from_core(rows), 0)
    project = jnp.swapaxes(project, 1, 2).reshape(1792, 512)
    basis = nt(start, inverse, HI).astype(BF16)

    wide = project.astype(F32)
    squares = jnp.sum(wide * wide, axis=0, keepdims=True)
    squares = jnp.sum(spread(squares, "tp", None, 16), axis=0)
    rms = jnp.sqrt(squares / DF + 1e-06)
    factor_t = (wide / rms).astype(BF16)
    chosen = (jnp.arange(512)[None, :] == 16 * fsdp + jnp.arange(16)[:, None]).astype(BF16)
    new_factor = nt(chosen, factor_t).astype(BF16)
    new_momentum = (blend.astype(F32) - 0.4 * nt(basis, project)).astype(BF16)
    new_weight = (
        weight.astype(F32) - 2.0 * math.sqrt(DM / DF) * nt(basis, factor_t)
    ).astype(BF16)
    return (new_momentum, new_weight, new_factor)


def solution(mesh):
    placed = (P("fsdp", "tp"), P("fsdp", "tp"), P("fsdp", "tp"), P("fsdp", "tp"))
    return jax.shard_map(
        local,
        mesh=mesh,
        in_specs=placed,
        out_specs=(P("fsdp", "tp"), P("fsdp", "tp"), P("fsdp", "tp")),
        check_vma=False,
    )
```

```python
import math

import jax
import jax.numpy as jnp
from jax import lax
from jax.experimental import pallas as pl
from jax.experimental.pallas import tpu as pltpu
from jax.sharding import PartitionSpec as P

DM = 8192
DF = 28672
Z = 16
HI = lax.Precision.HIGHEST
F32 = jnp.float32
BF16 = jnp.bfloat16
B = 128

DEEP = [[z * 2 + c for z in range(Z)] for c in range(2)]


def from_core(value):
    return lax.ppermute(value, "fsdp", [(i ^ 1, i) for i in range(2 * Z)])


def spread(value, axis, groups, size):
    return lax.all_to_all(
        jnp.broadcast_to(value, (size,) + value.shape), axis, 0, 0, axis_index_groups=groups
    )


def by_core(core, mine, other, axis):
    return jnp.stack(
        [jnp.where(core == 0, mine, other), jnp.where(core == 0, other, mine)], axis=axis
    )


def pick(array, place):
    return lax.dynamic_index_in_dim(array, place, 0, keepdims=False)


def factor_block(diag):
    sub = lax.broadcasted_iota(jnp.int32, (8, B), 0)
    lanes = lax.broadcasted_iota(jnp.int32, (8, B), 1)
    left = [diag[8 * i : 8 * i + 8] for i in range(B // 8)]
    right = [(lanes == sub + 8 * i).astype(F32) for i in range(B // 8)]
    done = []
    for p in range(B // 8):
        w, v = left[p], right[p]
        spread = lambda x, q: jnp.broadcast_to(x[:, 8 * p + q : 8 * p + q + 1], (8, B))
        full = lambda x, j: jnp.broadcast_to(x[j : j + 1], (8, B))
        cols = [spread(w, q) for q in range(8)]
        tri = {(i, q): full(cols[q], i) for q in range(8) for i in range(q, 8)}
        roots, above = [], {}
        for j in range(8):
            pivot = tri[j, j]
            root, inv = lax.rsqrt(pivot), pl.reciprocal(pivot, approx=True)
            roots.append(root)
            for q in range(j + 1, 8):
                for i in range(q, 8):
                    tri[i, q] = tri[i, q] - (tri[i, j] * tri[q, j]) * inv
            col = jnp.where(sub > j, cols[j] * root, 0.0)
            for q in range(j + 1, 8):
                above[j, q] = tri[q, j] * root
                cols[q] = cols[q] - col * above[j, q]
            row = full(w, j) * root
            w = jnp.where(sub == j, row, w - col * row)
            row = full(v, j) * root
            v = jnp.where(sub == j, row, v - col * row)
        done.append(v)
        for i in range(p + 1, B // 8):
            a, e = left[i], right[i]
            cols = [spread(a, q) for q in range(8)]
            for j in range(8):
                col = cols[j] * roots[j]
                for q in range(j + 1, 8):
                    cols[q] = cols[q] - col * above[j, q]
                a = a - col * w[j : j + 1]
                e = e - col * v[j : j + 1]
            left[i], right[i] = a, e
    return jnp.concatenate(done)


def inverse_kernel(gram_ref, out_ref, work):
    work[...] = gram_ref[...]
    out_ref[...] = jnp.zeros_like(out_ref)

    def dot(x, y, axis):
        return lax.dot_general(
            x, y, (((axis,), (0,)), ((), ())), precision=HI, preferred_element_type=F32
        )

    @pl.loop(0, 4)
    def _(b):
        at = pl.multiple_of(b * B, B)
        inv = factor_block(work[pl.ds(at, B), pl.ds(at, B)])

        for i in range(4):

            @pl.when(b == i)
            def _():
                here, rest, before = (
                    slice(i * B, i * B + B), slice(i * B + B, 512), slice(0, i * B)
                )
                out_ref[here, here] = inv
                if i > 0:
                    lower = dot(inv, out_ref[here, before], 1)
                    out_ref[here, before] = lower
                if i < 3:
                    upper = dot(inv, work[here, rest], 1)
                    work[rest, rest] = work[rest, rest] - dot(upper, upper, 0)
                    out_ref[rest, here] = -dot(upper, inv, 0)
                    if i > 0:
                        out_ref[rest, before] = out_ref[rest, before] - dot(upper, lower, 0)


def inverse_factor(gram):
    return pl.pallas_call(
        inverse_kernel,
        out_shape=jax.ShapeDtypeStruct((512, 512), F32),
        in_specs=[pl.BlockSpec(memory_space=pltpu.VMEM)],
        out_specs=pl.BlockSpec(memory_space=pltpu.VMEM),
        scratch_shapes=[pltpu.VMEM((512, 512), F32)],
        compiler_params=pltpu.CompilerParams(vmem_limit_bytes=24 * 1024 * 1024),
        cost_estimate=pl.CostEstimate(flops=6 * 10**8, bytes_accessed=3 * 2**20, transcendentals=512),
        name="inverse_factor",
    )(gram)


def nt(a, b, precision=None):
    return lax.dot_general(
        a, b, (((1,), (1,)), ((), ())), precision=precision, preferred_element_type=F32
    )


def tn(a, b):
    return lax.dot_general(a, b, (((0,), (0,)), ((), ())), preferred_element_type=F32)


def cross_kernel(place_ref, mine_ref, other_ref, start_ref, second_ref, cross_ref, band_ref):
    at = place_ref[0]
    rank = lax.broadcasted_iota(jnp.int32, (16, 512), 1)
    row = lax.broadcasted_iota(jnp.int32, (16, 512), 0)
    chosen = (rank == row + at).astype(F32)
    total, band = None, None
    for blend_ref, rows_ref in ((mine_ref, start_ref), (other_ref, second_ref)):
        rows = rows_ref[...]
        high = rows.astype(BF16)
        low = (rows - high.astype(F32)).astype(BF16)
        part = tn(blend_ref[...], high) + tn(blend_ref[...], low)
        total = part if total is None else total + part
        part = jnp.dot(nt(chosen, rows, HI), rows, precision=HI, preferred_element_type=F32)
        band = part if band is None else band + part
    cross_ref[...] = total
    band_ref[...] = band


def cross_and_band(place, mine, other, start, second):
    vmem = pl.BlockSpec(memory_space=pltpu.VMEM)
    return pl.pallas_call(
        cross_kernel,
        out_shape=(
            jax.ShapeDtypeStruct((mine.shape[1], 512), F32),
            jax.ShapeDtypeStruct((16, 512), F32),
        ),
        in_specs=[pl.BlockSpec(memory_space=pltpu.SMEM)] + [vmem] * 4,
        out_specs=(vmem, vmem),
        compiler_params=pltpu.CompilerParams(vmem_limit_bytes=32 * 1024 * 1024),
        cost_estimate=pl.CostEstimate(flops=10**9, bytes_accessed=4 * 2**20, transcendentals=0),
        name="cross_and_band",
    )(place, mine, other, start, second)


def local(momentum, gradient, weight, right_factor):
    fsdp, tp = lax.axis_index("fsdp"), lax.axis_index("tp")
    core = fsdp % 2

    blend = (momentum.astype(F32) + gradient.astype(F32)).astype(BF16)

    half = blend.shape[1] // 2
    columns = lambda place: lax.dynamic_slice_in_dim(blend, place * half, half, axis=1)
    mine, other = columns(core), from_core(columns(1 - core))

    rows = lax.all_gather(right_factor, "fsdp", axis_index_groups=DEEP)
    factor = by_core(core, rows, from_core(rows), 1).reshape(512, -1)
    partial = nt(blend, factor)
    pieces = lax.all_to_all(partial.reshape(16, 16, 512), "tp", 0, 0)
    start = spread(jnp.sum(pieces, axis=0), "tp", None, 16).reshape(256, 512)
    second = from_core(start)

    place = (16 * (2 * tp + core)).astype(jnp.int32).reshape(1)
    cross, band = cross_and_band(place, mine, other, start, second)
    cross = lax.psum_scatter(
        cross.reshape(16, 56, 512), "fsdp", scatter_dimension=0, axis_index_groups=DEEP
    )
    band = jnp.sum(lax.all_gather(band, "fsdp", axis_index_groups=DEEP), axis=0)
    bands = spread(band, "tp", None, 16)
    gram = by_core(core, bands, from_core(bands), 1).reshape(512, 512)

    inverse = inverse_factor(gram)
    chunk = nt(cross, inverse, HI).astype(BF16)
    rows = lax.all_gather(chunk, "fsdp", axis_index_groups=DEEP).reshape(-1, 512)
    basis = nt(start, inverse, HI).astype(BF16)

    wide = rows.astype(F32)
    squares = jnp.sum(wide * wide, axis=0, keepdims=True)
    squares = jnp.sum(spread(squares, "tp", None, 16), axis=0)
    squares = squares + from_core(squares)
    rms = jnp.sqrt(squares / DF + 1e-06)

    project = by_core(core, rows, from_core(rows), 0).reshape(-1, 512)
    chosen = jnp.arange(512)[None, :] == 16 * fsdp + jnp.arange(16)[:, None]
    new_factor = nt(chosen.astype(BF16), project)
    new_factor = new_factor / jnp.sum(jnp.where(chosen, rms, 0.0), axis=1, keepdims=True)
    factor_t = (project.astype(F32) / rms).astype(BF16)
    new_momentum = (blend.astype(F32) - 0.4 * nt(basis, project)).astype(BF16)
    new_weight = (
        weight.astype(F32) - 2.0 * math.sqrt(DM / DF) * nt(basis, factor_t)
    ).astype(BF16)
    return (new_momentum, new_weight, new_factor.astype(BF16))


def solution(mesh):
    placed = (P("fsdp", "tp"), P("fsdp", "tp"), P("fsdp", "tp"), P("fsdp", "tp"))
    return jax.shard_map(
        local,
        mesh=mesh,
        in_specs=placed,
        out_specs=(P("fsdp", "tp"), P("fsdp", "tp"), P("fsdp", "tp")),
        check_vma=False,
    )
```

```python
import math

import jax
import jax.numpy as jnp
from jax import lax
from jax.experimental import pallas as pl
from jax.experimental.pallas import tpu as pltpu
from jax.sharding import PartitionSpec as P

DM = 8192
DF = 28672
Z = 16
HI = lax.Precision.HIGHEST
F32 = jnp.float32
BF16 = jnp.bfloat16
B = 128

DEEP = [[z * 2 + c for z in range(Z)] for c in range(2)]


def from_core(value):
    return lax.ppermute(value, "fsdp", [(i ^ 1, i) for i in range(2 * Z)])


def spread(value, axis, groups, size):
    return lax.all_to_all(
        jnp.broadcast_to(value, (size,) + value.shape), axis, 0, 0, axis_index_groups=groups
    )


def by_core(core, mine, other, axis):
    return jnp.stack(
        [jnp.where(core == 0, mine, other), jnp.where(core == 0, other, mine)], axis=axis
    )


def pick(array, place):
    return lax.dynamic_index_in_dim(array, place, 0, keepdims=False)


def factor_block(diag):
    sub = lax.broadcasted_iota(jnp.int32, (8, B), 0)
    lanes = lax.broadcasted_iota(jnp.int32, (8, B), 1)
    left = [diag[8 * i : 8 * i + 8] for i in range(B // 8)]
    right = [(lanes == sub + 8 * i).astype(F32) for i in range(B // 8)]
    done = []
    for p in range(B // 8):
        w, v = left[p], right[p]
        spread = lambda x, q: jnp.broadcast_to(x[:, 8 * p + q : 8 * p + q + 1], (8, B))
        full = lambda x, j: jnp.broadcast_to(x[j : j + 1], (8, B))
        cols = [spread(w, q) for q in range(8)]
        roots, above = [], {}
        for j in range(0, 8, 2):
            k = j + 1
            first, cross, second = full(cols[j], j), full(cols[j], k), full(cols[k], k)
            inv = pl.reciprocal(first, approx=True)
            ratio = cross * inv
            schur = second - cross * ratio
            inv_schur = first * pl.reciprocal(first * second - cross * cross, approx=True)
            roots += [lax.rsqrt(first), lax.rsqrt(schur)]
            above[j, k] = cross * roots[j]
            next_col = cols[k] - cols[j] * ratio
            for q in range(k + 1, 8):
                top, low = full(cols[q], j), full(cols[q], k)
                low = low - ratio * top
                above[j, q], above[k, q] = top * roots[j], low * roots[k]
                cols[q] = (cols[q] - cols[j] * (top * inv)) - next_col * (low * inv_schur)
            for at, col in ((j, cols[j]), (k, next_col)):
                col = jnp.where(sub > at, col * roots[at], 0.0)
                row = full(w, at) * roots[at]
                w = jnp.where(sub == at, row, w - col * row)
                row = full(v, at) * roots[at]
                v = jnp.where(sub == at, row, v - col * row)
        done.append(v)
        for i in range(p + 1, B // 8):
            a, e = left[i], right[i]
            cols = [spread(a, q) for q in range(8)]
            for j in range(8):
                col = cols[j] * roots[j]
                for q in range(j + 1, 8):
                    cols[q] = cols[q] - col * above[j, q]
                a = a - col * w[j : j + 1]
                e = e - col * v[j : j + 1]
            left[i], right[i] = a, e
    return jnp.concatenate(done)


def inverse_kernel(gram_ref, out_ref, work):
    gram = gram_ref[...]
    diagonal = lax.broadcasted_iota(jnp.int32, (512, 512), 0) == lax.broadcasted_iota(
        jnp.int32, (512, 512), 1
    )
    only = jnp.where(diagonal, gram, 0.0)
    scale = lax.rsqrt(jnp.sum(only, axis=0, keepdims=True))
    work[...] = (gram * lax.rsqrt(jnp.sum(only, axis=1, keepdims=True))) * scale
    out_ref[...] = jnp.zeros_like(out_ref)

    def dot(x, y, axis):
        return lax.dot_general(
            x, y, (((axis,), (0,)), ((), ())), precision=HI, preferred_element_type=F32
        )

    @pl.loop(0, 4)
    def _(b):
        at = pl.multiple_of(b * B, B)
        inv = factor_block(work[pl.ds(at, B), pl.ds(at, B)])

        for i in range(4):

            @pl.when(b == i)
            def _():
                here, rest, before = (
                    slice(i * B, i * B + B), slice(i * B + B, 512), slice(0, i * B)
                )
                out_ref[here, here] = inv
                if i > 0:
                    lower = dot(inv, out_ref[here, before], 1)
                    out_ref[here, before] = lower
                if i < 3:
                    upper = dot(inv, work[here, rest], 1)
                    work[rest, rest] = work[rest, rest] - dot(upper, upper, 0)
                    out_ref[rest, here] = -dot(upper, inv, 0)
                    if i > 0:
                        out_ref[rest, before] = out_ref[rest, before] - dot(upper, lower, 0)

    out_ref[...] = out_ref[...] * scale


def inverse_factor(gram):
    return pl.pallas_call(
        inverse_kernel,
        out_shape=jax.ShapeDtypeStruct((512, 512), F32),
        in_specs=[pl.BlockSpec(memory_space=pltpu.VMEM)],
        out_specs=pl.BlockSpec(memory_space=pltpu.VMEM),
        scratch_shapes=[pltpu.VMEM((512, 512), F32)],
        compiler_params=pltpu.CompilerParams(vmem_limit_bytes=24 * 1024 * 1024),
        cost_estimate=pl.CostEstimate(flops=6 * 10**8, bytes_accessed=3 * 2**20, transcendentals=512),
        name="inverse_factor",
    )(gram)


def nt(a, b, precision=None):
    return lax.dot_general(
        a, b, (((1,), (1,)), ((), ())), precision=precision, preferred_element_type=F32
    )


def tn(a, b):
    return lax.dot_general(a, b, (((0,), (0,)), ((), ())), preferred_element_type=F32)


def cross_kernel(place_ref, mine_ref, other_ref, start_ref, second_ref, cross_ref, band_ref):
    at = place_ref[0]
    rank = lax.broadcasted_iota(jnp.int32, (16, 512), 1)
    row = lax.broadcasted_iota(jnp.int32, (16, 512), 0)
    chosen = (rank == row + at).astype(F32)
    total, band = None, None
    for blend_ref, rows_ref in ((mine_ref, start_ref), (other_ref, second_ref)):
        rows = rows_ref[...]
        high = rows.astype(BF16)
        low = (rows - high.astype(F32)).astype(BF16)
        part = tn(blend_ref[...], high) + tn(blend_ref[...], low)
        total = part if total is None else total + part
        part = jnp.dot(nt(chosen, rows, HI), rows, precision=HI, preferred_element_type=F32)
        band = part if band is None else band + part
    cross_ref[...] = total
    band_ref[...] = band


def cross_and_band(place, mine, other, start, second):
    vmem = pl.BlockSpec(memory_space=pltpu.VMEM)
    return pl.pallas_call(
        cross_kernel,
        out_shape=(
            jax.ShapeDtypeStruct((mine.shape[1], 512), F32),
            jax.ShapeDtypeStruct((16, 512), F32),
        ),
        in_specs=[pl.BlockSpec(memory_space=pltpu.SMEM)] + [vmem] * 4,
        out_specs=(vmem, vmem),
        compiler_params=pltpu.CompilerParams(vmem_limit_bytes=32 * 1024 * 1024),
        cost_estimate=pl.CostEstimate(flops=10**9, bytes_accessed=4 * 2**20, transcendentals=0),
        name="cross_and_band",
    )(place, mine, other, start, second)


def local(momentum, gradient, weight, right_factor):
    fsdp, tp = lax.axis_index("fsdp"), lax.axis_index("tp")
    core = fsdp % 2

    blend = (momentum.astype(F32) + gradient.astype(F32)).astype(BF16)

    half = blend.shape[1] // 2
    columns = lambda place: lax.dynamic_slice_in_dim(blend, place * half, half, axis=1)
    mine, other = columns(core), from_core(columns(1 - core))

    rows = lax.all_gather(right_factor, "fsdp", axis_index_groups=DEEP)
    factor = by_core(core, rows, from_core(rows), 1).reshape(512, -1)
    partial = nt(blend, factor)
    pieces = lax.all_to_all(partial.reshape(16, 16, 512), "tp", 0, 0)
    start = spread(jnp.sum(pieces, axis=0), "tp", None, 16).reshape(256, 512)
    start, other = lax.optimization_barrier((start, other))
    second = from_core(start)

    place = (16 * (2 * tp + core)).astype(jnp.int32).reshape(1)
    cross, band = cross_and_band(place, mine, other, start, second)
    cross = lax.psum_scatter(
        cross.reshape(16, 56, 512), "fsdp", scatter_dimension=0, axis_index_groups=DEEP
    )
    band = jnp.sum(lax.all_gather(band, "fsdp", axis_index_groups=DEEP), axis=0)
    bands = spread(band, "tp", None, 16)
    gram = by_core(core, bands, from_core(bands), 1).reshape(512, 512)

    inverse = inverse_factor(gram)
    chunk = nt(cross, inverse, HI).astype(BF16)
    rows = lax.all_gather(chunk, "fsdp", axis_index_groups=DEEP).reshape(-1, 512)
    basis = nt(start, inverse, HI).astype(BF16)

    wide = rows.astype(F32)
    squares = jnp.broadcast_to(jnp.sum(wide * wide, axis=0, keepdims=True), (16, 1, 512))
    rows, squares = lax.optimization_barrier((rows, squares))
    squares = lax.all_to_all(squares, "tp", 0, 0)
    project = by_core(core, rows, from_core(rows), 0).reshape(-1, 512)
    chosen = jnp.arange(512)[None, :] == 16 * fsdp + jnp.arange(16)[:, None]
    new_factor = nt(chosen.astype(BF16), project)
    new_momentum = (blend.astype(F32) - 0.4 * nt(basis, project)).astype(BF16)
    squares, new_momentum, new_factor = lax.optimization_barrier(
        (squares, new_momentum, new_factor)
    )
    squares = jnp.sum(squares, axis=0)
    squares = squares + from_core(squares)
    rms = jnp.sqrt(squares / DF + 1e-06)

    new_factor = new_factor / jnp.sum(jnp.where(chosen, rms, 0.0), axis=1, keepdims=True)
    factor_t = (project.astype(F32) / rms).astype(BF16)
    new_weight = (
        weight.astype(F32) - 2.0 * math.sqrt(DM / DF) * nt(basis, factor_t)
    ).astype(BF16)
    return (new_momentum, new_weight, new_factor.astype(BF16))


def solution(mesh):
    placed = (P("fsdp", "tp"), P("fsdp", "tp"), P("fsdp", "tp"), P("fsdp", "tp"))
    return jax.shard_map(
        local,
        mesh=mesh,
        in_specs=placed,
        out_specs=(P("fsdp", "tp"), P("fsdp", "tp"), P("fsdp", "tp")),
        check_vma=False,
    )
```

```python
import math

import jax
import jax.numpy as jnp
from jax import lax
from jax.experimental import pallas as pl
from jax.experimental.pallas import tpu as pltpu
from jax.sharding import PartitionSpec as P

DM = 8192
DF = 28672
Z = 16
HI = lax.Precision.HIGHEST
F32 = jnp.float32
BF16 = jnp.bfloat16
B = 128

DEEP = [[z * 2 + c for z in range(Z)] for c in range(2)]


def from_core(value):
    return lax.ppermute(value, "fsdp", [(i ^ 1, i) for i in range(2 * Z)])


def spread(value, axis, groups, size):
    return lax.all_to_all(
        jnp.broadcast_to(value, (size,) + value.shape), axis, 0, 0, axis_index_groups=groups
    )


def by_core(core, mine, other, axis):
    return jnp.stack(
        [jnp.where(core == 0, mine, other), jnp.where(core == 0, other, mine)], axis=axis
    )


def pick(array, place):
    return lax.dynamic_index_in_dim(array, place, 0, keepdims=False)


def factor_block(diag):
    sub = lax.broadcasted_iota(jnp.int32, (8, B), 0)
    lanes = lax.broadcasted_iota(jnp.int32, (8, B), 1)
    left = [diag[8 * i : 8 * i + 8] for i in range(B // 8)]
    right = [(lanes == sub + 8 * i).astype(F32) for i in range(B // 8)]
    done = []
    full = lambda x, j: jnp.broadcast_to(x[j : j + 1], (8, B))

    def spread(x, at):
        return jnp.broadcast_to(x[:, at : at + 1], (8, B))

    cols = [spread(left[0], q) for q in range(8)]
    for p in range(B // 8):
        inv, unit, pivots = [], {}, []
        for j in range(0, 8, 2):
            k = j + 1
            first, cross, second = full(cols[j], j), full(cols[j], k), full(cols[k], k)
            inv_first = pl.reciprocal(first, approx=True)
            unit[k, j] = cross * inv_first
            inv += [
                inv_first,
                first * pl.reciprocal(first * second - cross * cross, approx=True),
            ]
            pivots += [first, second - cross * unit[k, j]]
            cols[k] = cols[k] - cols[j] * unit[k, j]
            for q in range(k + 1, 8):
                top, low = full(cols[q], j), full(cols[q], k)
                unit[q, j] = top * inv[j]
                unit[q, k] = (low - unit[k, j] * top) * inv[k]
                cols[q] = (cols[q] - cols[j] * unit[q, j]) - cols[k] * unit[q, k]

        def columns(block):
            c = [spread(block, 8 * p + q) for q in range(8)]
            for q in range(1, 8):
                for j in range(q):
                    c[q] = c[q] - c[j] * unit[q, j]
            return c, [c[q] * inv[q] for q in range(8)]

        if p + 1 < B // 8:
            below, scaled = columns(left[p + 1])
            for_next = [spread(left[p + 1], 8 * (p + 1) + q) for q in range(8)]
            for q in range(8):
                for j in range(8):
                    for_next[q] = for_next[q] - scaled[j] * full(below[j], q)

        lower = [jnp.where(sub > j, cols[j] * inv[j], 0.0) for j in range(7)]
        w = v = None
        for c in range(8):
            t = (sub == c).astype(F32)
            if c < 7:
                t = t - lower[c]
            for j in range(c + 1, 7):
                t = t - lower[j] * full(t, j)
            dw, dv = t * full(left[p], c), t * full(right[p], c)
            w, v = (dw, dv) if c == 0 else (w + dw, v + dv)
        pivot = pivots[0]
        for j in range(1, 8):
            pivot = jnp.where(sub == j, pivots[j], pivot)
        done.append(v * lax.rsqrt(pivot))

        for i in range(p + 1, B // 8):
            if i > p + 1:
                _, scaled = columns(left[i])
            a, e = left[i], right[i]
            for j in range(8):
                a = a - scaled[j] * w[j : j + 1]
                e = e - scaled[j] * v[j : j + 1]
            left[i], right[i] = a, e
        if p + 1 < B // 8:
            cols = for_next
    return jnp.concatenate(done)


def inverse_kernel(gram_ref, out_ref, work):
    gram = gram_ref[...]
    diagonal = lax.broadcasted_iota(jnp.int32, (512, 512), 0) == lax.broadcasted_iota(
        jnp.int32, (512, 512), 1
    )
    only = jnp.where(diagonal, gram, 0.0)
    scale = lax.rsqrt(jnp.sum(only, axis=0, keepdims=True))
    work[...] = (gram * lax.rsqrt(jnp.sum(only, axis=1, keepdims=True))) * scale
    out_ref[...] = jnp.zeros_like(out_ref)

    def dot(x, y, axis):
        return lax.dot_general(
            x, y, (((axis,), (0,)), ((), ())), precision=HI, preferred_element_type=F32
        )

    @pl.loop(0, 4)
    def _(b):
        at = pl.multiple_of(b * B, B)
        inv = factor_block(work[pl.ds(at, B), pl.ds(at, B)])

        for i in range(4):

            @pl.when(b == i)
            def _():
                here, rest, before = (
                    slice(i * B, i * B + B), slice(i * B + B, 512), slice(0, i * B)
                )
                out_ref[here, here] = inv
                if i > 0:
                    lower = dot(inv, out_ref[here, before], 1)
                    out_ref[here, before] = lower
                if i < 3:
                    upper = dot(inv, work[here, rest], 1)
                    work[rest, rest] = work[rest, rest] - dot(upper, upper, 0)
                    out_ref[rest, here] = -dot(upper, inv, 0)
                    if i > 0:
                        out_ref[rest, before] = out_ref[rest, before] - dot(upper, lower, 0)

    out_ref[...] = out_ref[...] * scale


def inverse_factor(gram):
    return pl.pallas_call(
        inverse_kernel,
        out_shape=jax.ShapeDtypeStruct((512, 512), F32),
        in_specs=[pl.BlockSpec(memory_space=pltpu.VMEM)],
        out_specs=pl.BlockSpec(memory_space=pltpu.VMEM),
        scratch_shapes=[pltpu.VMEM((512, 512), F32)],
        compiler_params=pltpu.CompilerParams(vmem_limit_bytes=12 * 2**20),
        cost_estimate=pl.CostEstimate(flops=6 * 10**8, bytes_accessed=3 * 2**20, transcendentals=512),
        name="inverse_factor",
    )(gram)


def nt(a, b, precision=None):
    return lax.dot_general(
        a, b, (((1,), (1,)), ((), ())), precision=precision, preferred_element_type=F32
    )


def tn(a, b):
    return lax.dot_general(a, b, (((0,), (0,)), ((), ())), preferred_element_type=F32)


def cross_kernel(place_ref, mine_ref, other_ref, start_ref, second_ref, cross_ref, band_ref):
    at = place_ref[0]
    rank = lax.broadcasted_iota(jnp.int32, (16, 512), 1)
    row = lax.broadcasted_iota(jnp.int32, (16, 512), 0)
    chosen = (rank == row + at).astype(F32)
    total, band = None, None
    for blend_ref, rows_ref in ((mine_ref, start_ref), (other_ref, second_ref)):
        rows = rows_ref[...]
        high = rows.astype(BF16)
        low = (rows - high.astype(F32)).astype(BF16)
        part = tn(blend_ref[...], high) + tn(blend_ref[...], low)
        total = part if total is None else total + part
        part = jnp.dot(nt(chosen, rows, HI), rows, precision=HI, preferred_element_type=F32)
        band = part if band is None else band + part
    cross_ref[...] = total
    band_ref[...] = band


def cross_and_band(place, mine, other, start, second):
    vmem = pl.BlockSpec(memory_space=pltpu.VMEM)
    return pl.pallas_call(
        cross_kernel,
        out_shape=(
            jax.ShapeDtypeStruct((mine.shape[1], 512), F32),
            jax.ShapeDtypeStruct((16, 512), F32),
        ),
        in_specs=[pl.BlockSpec(memory_space=pltpu.SMEM)] + [vmem] * 4,
        out_specs=(vmem, vmem),
        compiler_params=pltpu.CompilerParams(vmem_limit_bytes=16 * 2**20),
        cost_estimate=pl.CostEstimate(flops=10**9, bytes_accessed=4 * 2**20, transcendentals=0),
        name="cross_and_band",
    )(place, mine, other, start, second)


def half_columns(place):
    return pl.ds(pl.multiple_of(place * 896, 128), 896)


def feedback_kernel(core_ref, rows_ref, other_ref, basis_ref, blend_ref, out_ref):
    basis = basis_ref[...]
    for place, project_ref in ((core_ref[0], rows_ref), (1 - core_ref[0], other_ref)):
        at = half_columns(place)
        product = nt(basis, project_ref[...])
        out_ref[:, at] = (blend_ref[:, at].astype(F32) - 0.4 * product).astype(BF16)


def update_kernel(
    at_ref, squares_ref, rows_ref, other_ref, basis_ref, weight_ref, out_ref, factor_ref
):
    basis = basis_ref[...]
    squares = jnp.sum(squares_ref[...], axis=0, keepdims=True)
    rms = jnp.sqrt(squares / DF + 1e-06)
    rank = lax.broadcasted_iota(jnp.int32, (16, 512), 1)
    row = lax.broadcasted_iota(jnp.int32, (16, 512), 0)
    chosen = (rank == row + at_ref[1]).astype(BF16)
    for place, project_ref in ((at_ref[0], rows_ref), (1 - at_ref[0], other_ref)):
        at = half_columns(place)
        factor = (project_ref[...].astype(F32) / rms).astype(BF16)
        product = nt(basis, factor)
        step = 2.0 * math.sqrt(DM / DF) * product
        out_ref[:, at] = (weight_ref[:, at].astype(F32) - step).astype(BF16)
        factor_ref[:, at] = nt(chosen, factor).astype(BF16)


def tail_call(kernel, name, flops, out_rows, *operands):
    vmem = pl.BlockSpec(memory_space=pltpu.VMEM)
    return pl.pallas_call(
        kernel,
        out_shape=tuple(jax.ShapeDtypeStruct((n, 1792), BF16) for n in out_rows),
        in_specs=[pl.BlockSpec(memory_space=pltpu.SMEM)] + [vmem] * (len(operands) - 1),
        out_specs=(vmem,) * len(out_rows),
        compiler_params=pltpu.CompilerParams(vmem_limit_bytes=16 * 2**20),
        cost_estimate=pl.CostEstimate(flops=flops, bytes_accessed=4 * 2**20, transcendentals=0),
        name=name,
    )(*operands)


def local(momentum, gradient, weight, right_factor):
    fsdp, tp = lax.axis_index("fsdp"), lax.axis_index("tp")
    core = fsdp % 2

    blend = (momentum.astype(F32) + gradient.astype(F32)).astype(BF16)

    half = blend.shape[1] // 2
    columns = lambda place: lax.dynamic_slice_in_dim(blend, place * half, half, axis=1)
    mine, other = columns(core), from_core(columns(1 - core))

    rows = lax.all_gather(right_factor, "fsdp", axis_index_groups=DEEP)
    factor = by_core(core, rows, from_core(rows), 1).reshape(512, -1)
    partial = nt(blend, factor)
    pieces = lax.all_to_all(partial.reshape(16, 16, 512), "tp", 0, 0)
    start = spread(jnp.sum(pieces, axis=0), "tp", None, 16).reshape(256, 512)
    start, other = lax.optimization_barrier((start, other))
    second = from_core(start)

    place = (16 * (2 * tp + core)).astype(jnp.int32).reshape(1)
    cross, band = cross_and_band(place, mine, other, start, second)
    cross = lax.psum_scatter(
        cross.reshape(16, 56, 512), "fsdp", scatter_dimension=0, axis_index_groups=DEEP
    )
    band = jnp.sum(lax.all_gather(band, "fsdp", axis_index_groups=DEEP), axis=0)
    bands = spread(band, "tp", None, 16)
    gram = by_core(core, bands, from_core(bands), 1).reshape(512, 512)

    inverse = inverse_factor(gram)
    chunk = nt(cross, inverse, HI).astype(BF16)
    rows = lax.all_gather(chunk, "fsdp", axis_index_groups=DEEP).reshape(-1, 512)
    other = from_core(rows)

    total = lambda half: jnp.sum(jnp.square(half.astype(F32)), axis=0)
    squares = jnp.broadcast_to(total(rows) + total(other), (16, 1, 512))
    squares, start = lax.optimization_barrier((squares, start))
    basis = nt(start, inverse, HI).astype(BF16)
    squares = lax.all_to_all(squares, "tp", 0, 0)
    place = jnp.stack([core, 16 * fsdp]).astype(jnp.int32)
    (new_momentum,) = tail_call(
        feedback_kernel, "feedback", 5 * 10**8, (256,), place, rows, other, basis, blend
    )
    squares, new_momentum = lax.optimization_barrier((squares, new_momentum))
    new_weight, new_factor = tail_call(
        update_kernel, "update", 5 * 10**8, (256, 16),
        place, squares.reshape(16, 512), rows, other, basis, weight,
    )
    return (new_momentum, new_weight, new_factor)


def solution(mesh):
    placed = (P("fsdp", "tp"), P("fsdp", "tp"), P("fsdp", "tp"), P("fsdp", "tp"))
    return jax.shard_map(
        local,
        mesh=mesh,
        in_specs=placed,
        out_specs=(P("fsdp", "tp"), P("fsdp", "tp"), P("fsdp", "tp")),
        check_vma=False,
    )
```

```python
import math

import jax
import jax.numpy as jnp
from jax import lax
from jax.experimental import pallas as pl
from jax.experimental.pallas import tpu as pltpu
from jax.sharding import PartitionSpec as P

DM = 8192
DF = 28672
Z = 16
HI = lax.Precision.HIGHEST
F32 = jnp.float32
BF16 = jnp.bfloat16
B = 128

DEEP = [[z * 2 + ((z + g) % 2) for z in range(Z)] for g in range(2)]


def from_core(value):
    return lax.ppermute(value, "fsdp", [(i ^ 1, i) for i in range(2 * Z)])


def spread(value, axis, groups, size):
    return lax.all_to_all(
        jnp.broadcast_to(value, (size,) + value.shape), axis, 0, 0, axis_index_groups=groups
    )


def by_group(group, mine, other, axis):
    return jnp.stack(
        [jnp.where(group == 0, mine, other), jnp.where(group == 0, other, mine)], axis=axis
    )


def pick(array, place):
    return lax.dynamic_index_in_dim(array, place, 0, keepdims=False)


def factor_block(diag):
    sub = lax.broadcasted_iota(jnp.int32, (8, B), 0)
    lanes = lax.broadcasted_iota(jnp.int32, (8, B), 1)
    left = [diag[8 * i : 8 * i + 8] for i in range(B // 8)]
    right = [(lanes == sub + 8 * i).astype(F32) for i in range(B // 8)]
    done = []
    full = lambda x, j: jnp.broadcast_to(x[j : j + 1], (8, B))

    def spread(x, at):
        return jnp.broadcast_to(x[:, at : at + 1], (8, B))

    cols = [spread(left[0], q) for q in range(8)]
    for p in range(B // 8):
        inv, unit, pivots = [], {}, []
        for j in range(0, 8, 2):
            k = j + 1
            first, cross, second = full(cols[j], j), full(cols[j], k), full(cols[k], k)
            inv_first = pl.reciprocal(first, approx=True)
            unit[k, j] = cross * inv_first
            inv += [
                inv_first,
                first * pl.reciprocal(first * second - cross * cross, approx=True),
            ]
            pivots += [first, second - cross * unit[k, j]]
            cols[k] = cols[k] - cols[j] * unit[k, j]
            for q in range(k + 1, 8):
                top, low = full(cols[q], j), full(cols[q], k)
                unit[q, j] = top * inv[j]
                unit[q, k] = (low - unit[k, j] * top) * inv[k]
                cols[q] = (cols[q] - cols[j] * unit[q, j]) - cols[k] * unit[q, k]

        def columns(block):
            c = [spread(block, 8 * p + q) for q in range(8)]
            for q in range(1, 8):
                for j in range(q):
                    c[q] = c[q] - c[j] * unit[q, j]
            return c, [c[q] * inv[q] for q in range(8)]

        if p + 1 < B // 8:
            below, scaled = columns(left[p + 1])
            for_next = [spread(left[p + 1], 8 * (p + 1) + q) for q in range(8)]
            for q in range(8):
                for j in range(8):
                    for_next[q] = for_next[q] - scaled[j] * full(below[j], q)

        lower = [jnp.where(sub > j, cols[j] * inv[j], 0.0) for j in range(7)]
        w = v = None
        for c in range(8):
            t = (sub == c).astype(F32)
            if c < 7:
                t = t - lower[c]
            for j in range(c + 1, 7):
                t = t - lower[j] * full(t, j)
            dw, dv = t * full(left[p], c), t * full(right[p], c)
            w, v = (dw, dv) if c == 0 else (w + dw, v + dv)
        pivot = pivots[0]
        for j in range(1, 8):
            pivot = jnp.where(sub == j, pivots[j], pivot)
        done.append(v * lax.rsqrt(pivot))

        for i in range(p + 1, B // 8):
            if i > p + 1:
                _, scaled = columns(left[i])
            a, e = left[i], right[i]
            for j in range(8):
                a = a - scaled[j] * w[j : j + 1]
                e = e - scaled[j] * v[j : j + 1]
            left[i], right[i] = a, e
        if p + 1 < B // 8:
            cols = for_next
    return jnp.concatenate(done)


def inverse_kernel(gram_ref, out_ref, work):
    gram = gram_ref[...]
    diagonal = lax.broadcasted_iota(jnp.int32, (512, 512), 0) == lax.broadcasted_iota(
        jnp.int32, (512, 512), 1
    )
    only = jnp.where(diagonal, gram, 0.0)
    scale = lax.rsqrt(jnp.sum(only, axis=0, keepdims=True))
    work[...] = (gram * lax.rsqrt(jnp.sum(only, axis=1, keepdims=True))) * scale
    out_ref[...] = jnp.zeros_like(out_ref)

    def dot(x, y, axis):
        return lax.dot_general(
            x, y, (((axis,), (0,)), ((), ())), precision=HI, preferred_element_type=F32
        )

    @pl.loop(0, 4)
    def _(b):
        at = pl.multiple_of(b * B, B)
        inv = factor_block(work[pl.ds(at, B), pl.ds(at, B)])

        for i in range(4):

            @pl.when(b == i)
            def _():
                here, rest, before = (
                    slice(i * B, i * B + B), slice(i * B + B, 512), slice(0, i * B)
                )
                out_ref[here, here] = inv
                if i > 0:
                    lower = dot(inv, out_ref[here, before], 1)
                    out_ref[here, before] = lower
                if i < 3:
                    upper = dot(inv, work[here, rest], 1)
                    work[rest, rest] = work[rest, rest] - dot(upper, upper, 0)
                    out_ref[rest, here] = -dot(upper, inv, 0)
                    if i > 0:
                        out_ref[rest, before] = out_ref[rest, before] - dot(upper, lower, 0)

    out_ref[...] = out_ref[...] * scale


def inverse_factor(gram):
    return pl.pallas_call(
        inverse_kernel,
        out_shape=jax.ShapeDtypeStruct((512, 512), F32),
        in_specs=[pl.BlockSpec(memory_space=pltpu.VMEM)],
        out_specs=pl.BlockSpec(memory_space=pltpu.VMEM),
        scratch_shapes=[pltpu.VMEM((512, 512), F32)],
        compiler_params=pltpu.CompilerParams(vmem_limit_bytes=12 * 2**20),
        cost_estimate=pl.CostEstimate(flops=6 * 10**8, bytes_accessed=3 * 2**20, transcendentals=512),
        name="inverse_factor",
    )(gram)


def nt(a, b, precision=None):
    return lax.dot_general(
        a, b, (((1,), (1,)), ((), ())), precision=precision, preferred_element_type=F32
    )


def tn(a, b):
    return lax.dot_general(a, b, (((0,), (0,)), ((), ())), preferred_element_type=F32)


def cross_kernel(place_ref, mine_ref, other_ref, start_ref, second_ref, cross_ref, band_ref):
    at = place_ref[0]
    rank = lax.broadcasted_iota(jnp.int32, (16, 512), 1)
    row = lax.broadcasted_iota(jnp.int32, (16, 512), 0)
    chosen = (rank == row + at).astype(F32)
    total, band = None, None
    for blend_ref, rows_ref in ((mine_ref, start_ref), (other_ref, second_ref)):
        rows = rows_ref[...]
        high = rows.astype(BF16)
        low = (rows - high.astype(F32)).astype(BF16)
        part = tn(blend_ref[...], high) + tn(blend_ref[...], low)
        total = part if total is None else total + part
        part = jnp.dot(nt(chosen, rows, HI), rows, precision=HI, preferred_element_type=F32)
        band = part if band is None else band + part
    cross_ref[...] = total
    band_ref[...] = band


def cross_and_band(place, mine, other, start, second):
    vmem = pl.BlockSpec(memory_space=pltpu.VMEM)
    return pl.pallas_call(
        cross_kernel,
        out_shape=(
            jax.ShapeDtypeStruct((mine.shape[1], 512), F32),
            jax.ShapeDtypeStruct((16, 512), F32),
        ),
        in_specs=[pl.BlockSpec(memory_space=pltpu.SMEM)] + [vmem] * 4,
        out_specs=(vmem, vmem),
        compiler_params=pltpu.CompilerParams(vmem_limit_bytes=16 * 2**20),
        cost_estimate=pl.CostEstimate(flops=10**9, bytes_accessed=4 * 2**20, transcendentals=0),
        name="cross_and_band",
    )(place, mine, other, start, second)


def half_columns(place):
    return pl.ds(pl.multiple_of(place * 896, 128), 896)


def feedback_kernel(core_ref, rows_ref, other_ref, basis_ref, blend_ref, out_ref):
    basis = basis_ref[...]
    for place, project_ref in ((core_ref[0], rows_ref), (1 - core_ref[0], other_ref)):
        at = half_columns(place)
        product = nt(basis, project_ref[...])
        out_ref[:, at] = (blend_ref[:, at].astype(F32) - 0.4 * product).astype(BF16)


def update_kernel(
    at_ref, squares_ref, rows_ref, other_ref, basis_ref, weight_ref, out_ref, factor_ref
):
    basis = basis_ref[...]
    squares = jnp.sum(squares_ref[...], axis=0, keepdims=True)
    rms = jnp.sqrt(squares / DF + 1e-06)
    rank = lax.broadcasted_iota(jnp.int32, (16, 512), 1)
    row = lax.broadcasted_iota(jnp.int32, (16, 512), 0)
    chosen = (rank == row + at_ref[1]).astype(BF16)
    for place, project_ref in ((at_ref[0], rows_ref), (1 - at_ref[0], other_ref)):
        at = half_columns(place)
        factor = (project_ref[...].astype(F32) / rms).astype(BF16)
        product = nt(basis, factor)
        step = 2.0 * math.sqrt(DM / DF) * product
        out_ref[:, at] = (weight_ref[:, at].astype(F32) - step).astype(BF16)
        factor_ref[:, at] = nt(chosen, factor).astype(BF16)


def tail_call(kernel, name, flops, out_rows, *operands):
    vmem = pl.BlockSpec(memory_space=pltpu.VMEM)
    return pl.pallas_call(
        kernel,
        out_shape=tuple(jax.ShapeDtypeStruct((n, 1792), BF16) for n in out_rows),
        in_specs=[pl.BlockSpec(memory_space=pltpu.SMEM)] + [vmem] * (len(operands) - 1),
        out_specs=(vmem,) * len(out_rows),
        compiler_params=pltpu.CompilerParams(vmem_limit_bytes=16 * 2**20),
        cost_estimate=pl.CostEstimate(flops=flops, bytes_accessed=4 * 2**20, transcendentals=0),
        name=name,
    )(*operands)


def local(momentum, gradient, weight, right_factor):
    fsdp, tp = lax.axis_index("fsdp"), lax.axis_index("tp")
    group = (fsdp + fsdp // 2) % 2

    blend = (momentum.astype(F32) + gradient.astype(F32)).astype(BF16)

    half = blend.shape[1] // 2
    columns = lambda place: lax.dynamic_slice_in_dim(blend, place * half, half, axis=1)
    mine, other = columns(group), from_core(columns(1 - group))

    rows = lax.all_gather(right_factor, "fsdp", axis_index_groups=DEEP)
    others = from_core(rows)
    first = (jnp.arange(Z) + group)[:, None, None] % 2 == 0
    factor = jnp.stack([jnp.where(first, rows, others), jnp.where(first, others, rows)], axis=1)
    factor = factor.reshape(512, -1)
    partial = nt(blend, factor)
    pieces = lax.all_to_all(partial.reshape(16, 16, 512), "tp", 0, 0)
    start = spread(jnp.sum(pieces, axis=0), "tp", None, 16).reshape(256, 512)
    start, other = lax.optimization_barrier((start, other))
    second = from_core(start)

    place = (16 * (2 * tp + group)).astype(jnp.int32).reshape(1)
    cross, band = cross_and_band(place, mine, other, start, second)
    cross = lax.psum_scatter(
        cross.reshape(16, 56, 512), "fsdp", scatter_dimension=0, axis_index_groups=DEEP
    )
    band = jnp.sum(lax.all_gather(band, "fsdp", axis_index_groups=DEEP), axis=0)
    bands = spread(band, "tp", None, 16)
    gram = by_group(group, bands, from_core(bands), 1).reshape(512, 512)

    inverse = inverse_factor(gram)
    chunk = nt(cross, inverse, HI).astype(BF16)
    rows = lax.all_gather(chunk, "fsdp", axis_index_groups=DEEP).reshape(-1, 512)
    other = from_core(rows)

    total = lambda half: jnp.sum(jnp.square(half.astype(F32)), axis=0)
    squares = jnp.broadcast_to(total(rows) + total(other), (16, 1, 512))
    squares, start = lax.optimization_barrier((squares, start))
    basis = nt(start, inverse, HI).astype(BF16)
    squares = lax.all_to_all(squares, "tp", 0, 0)
    place = jnp.stack([group, 16 * fsdp]).astype(jnp.int32)
    (new_momentum,) = tail_call(
        feedback_kernel, "feedback", 5 * 10**8, (256,), place, rows, other, basis, blend
    )
    squares, new_momentum = lax.optimization_barrier((squares, new_momentum))
    new_weight, new_factor = tail_call(
        update_kernel, "update", 5 * 10**8, (256, 16),
        place, squares.reshape(16, 512), rows, other, basis, weight,
    )
    return (new_momentum, new_weight, new_factor)


def solution(mesh):
    placed = (P("fsdp", "tp"), P("fsdp", "tp"), P("fsdp", "tp"), P("fsdp", "tp"))
    return jax.shard_map(
        local,
        mesh=mesh,
        in_specs=placed,
        out_specs=(P("fsdp", "tp"), P("fsdp", "tp"), P("fsdp", "tp")),
        check_vma=False,
    )
```

```python
import math

import jax
import jax.numpy as jnp
from jax import lax
from jax.experimental import pallas as pl
from jax.experimental.pallas import tpu as pltpu
from jax.sharding import PartitionSpec as P

DM = 8192
DF = 28672
Z = 16
HI = lax.Precision.HIGHEST
F32 = jnp.float32
BF16 = jnp.bfloat16
B = 128

DEEP = [[z * 2 + ((z + g) % 2) for z in range(Z)] for g in range(2)]


def from_core(value):
    return lax.ppermute(value, "fsdp", [(i ^ 1, i) for i in range(2 * Z)])


def spread(value, axis, groups, size):
    return lax.all_to_all(
        jnp.broadcast_to(value, (size,) + value.shape), axis, 0, 0, axis_index_groups=groups
    )


def by_group(group, mine, other, axis):
    return jnp.stack(
        [jnp.where(group == 0, mine, other), jnp.where(group == 0, other, mine)], axis=axis
    )


def pick(array, place):
    return lax.dynamic_index_in_dim(array, place, 0, keepdims=False)


def factor_block(diag):
    sub = lax.broadcasted_iota(jnp.int32, (8, B), 0)
    lanes = lax.broadcasted_iota(jnp.int32, (8, B), 1)
    left = [diag[8 * i : 8 * i + 8] for i in range(B // 8)]
    right = [(lanes == sub + 8 * i).astype(F32) for i in range(B // 8)]
    done = []
    full = lambda x, j: jnp.broadcast_to(x[j : j + 1], (8, B))

    def spread(x, at):
        return jnp.broadcast_to(x[:, at : at + 1], (8, B))

    cols = [spread(left[0], q) for q in range(8)]
    for p in range(B // 8):
        inv, unit, pivots = [], {}, []
        for j in range(0, 8, 2):
            k = j + 1
            first, cross, second = full(cols[j], j), full(cols[j], k), full(cols[k], k)
            inv_first = pl.reciprocal(first, approx=True)
            unit[k, j] = cross * inv_first
            inv += [
                inv_first,
                first * pl.reciprocal(first * second - cross * cross, approx=True),
            ]
            pivots += [first, second - cross * unit[k, j]]
            cols[k] = cols[k] - cols[j] * unit[k, j]
            for q in range(k + 1, 8):
                top, low = full(cols[q], j), full(cols[q], k)
                unit[q, j] = top * inv[j]
                unit[q, k] = (low - unit[k, j] * top) * inv[k]
                cols[q] = (cols[q] - cols[j] * unit[q, j]) - cols[k] * unit[q, k]

        def columns(block):
            c = [spread(block, 8 * p + q) for q in range(8)]
            for q in range(1, 8):
                for j in range(q):
                    c[q] = c[q] - c[j] * unit[q, j]
            return c, [c[q] * inv[q] for q in range(8)]

        if p + 1 < B // 8:
            below, scaled = columns(left[p + 1])
            for_next = [spread(left[p + 1], 8 * (p + 1) + q) for q in range(8)]
            for q in range(8):
                for j in range(8):
                    for_next[q] = for_next[q] - scaled[j] * full(below[j], q)

        lower = [jnp.where(sub > j, cols[j] * inv[j], 0.0) for j in range(7)]
        w = v = None
        for c in range(8):
            t = (sub == c).astype(F32)
            if c < 7:
                t = t - lower[c]
            for j in range(c + 1, 7):
                t = t - lower[j] * full(t, j)
            dw, dv = t * full(left[p], c), t * full(right[p], c)
            w, v = (dw, dv) if c == 0 else (w + dw, v + dv)
        pivot = pivots[0]
        for j in range(1, 8):
            pivot = jnp.where(sub == j, pivots[j], pivot)
        done.append(v * lax.rsqrt(pivot))

        for i in range(p + 1, B // 8):
            if i > p + 1:
                _, scaled = columns(left[i])
            a, e = left[i], right[i]
            for j in range(8):
                a = a - scaled[j] * w[j : j + 1]
                e = e - scaled[j] * v[j : j + 1]
            left[i], right[i] = a, e
        if p + 1 < B // 8:
            cols = for_next
    return jnp.concatenate(done)


def inverse_kernel(gram_ref, out_ref, work):
    gram = gram_ref[...]
    diagonal = lax.broadcasted_iota(jnp.int32, (512, 512), 0) == lax.broadcasted_iota(
        jnp.int32, (512, 512), 1
    )
    only = jnp.where(diagonal, gram, 0.0)
    scale = lax.rsqrt(jnp.sum(only, axis=0, keepdims=True))
    work[...] = (gram * lax.rsqrt(jnp.sum(only, axis=1, keepdims=True))) * scale
    out_ref[...] = jnp.zeros_like(out_ref)

    def dot(x, y, axis):
        return lax.dot_general(
            x, y, (((axis,), (0,)), ((), ())), precision=HI, preferred_element_type=F32
        )

    @pl.loop(0, 4)
    def _(b):
        at = pl.multiple_of(b * B, B)
        inv = factor_block(work[pl.ds(at, B), pl.ds(at, B)])

        for i in range(4):

            @pl.when(b == i)
            def _():
                here, rest, before = (
                    slice(i * B, i * B + B), slice(i * B + B, 512), slice(0, i * B)
                )
                out_ref[here, here] = inv
                if i > 0:
                    lower = dot(inv, out_ref[here, before], 1)
                    out_ref[here, before] = lower
                if i < 3:
                    upper = dot(inv, work[here, rest], 1)
                    work[rest, rest] = work[rest, rest] - dot(upper, upper, 0)
                    out_ref[rest, here] = -dot(upper, inv, 0)
                    if i > 0:
                        out_ref[rest, before] = out_ref[rest, before] - dot(upper, lower, 0)

    out_ref[...] = out_ref[...] * scale


def inverse_factor(gram):
    return pl.pallas_call(
        inverse_kernel,
        out_shape=jax.ShapeDtypeStruct((512, 512), F32),
        in_specs=[pl.BlockSpec(memory_space=pltpu.VMEM)],
        out_specs=pl.BlockSpec(memory_space=pltpu.VMEM),
        scratch_shapes=[pltpu.VMEM((512, 512), F32)],
        compiler_params=pltpu.CompilerParams(vmem_limit_bytes=12 * 2**20),
        cost_estimate=pl.CostEstimate(flops=6 * 10**8, bytes_accessed=3 * 2**20, transcendentals=512),
        name="inverse_factor",
    )(gram)


def nt(a, b, precision=None):
    return lax.dot_general(
        a, b, (((1,), (1,)), ((), ())), precision=precision, preferred_element_type=F32
    )


def tn(a, b):
    return lax.dot_general(a, b, (((0,), (0,)), ((), ())), preferred_element_type=F32)


def cross_kernel(place_ref, mine_ref, other_ref, start_ref, second_ref, cross_ref, band_ref):
    at = place_ref[0]
    rank = lax.broadcasted_iota(jnp.int32, (16, 512), 1)
    row = lax.broadcasted_iota(jnp.int32, (16, 512), 0)
    chosen = (rank == row + at).astype(F32)
    total, band = None, None
    for blend_ref, rows_ref in ((mine_ref, start_ref), (other_ref, second_ref)):
        rows = rows_ref[...]
        high = rows.astype(BF16)
        low = (rows - high.astype(F32)).astype(BF16)
        part = tn(blend_ref[...], high) + tn(blend_ref[...], low)
        total = part if total is None else total + part
        part = jnp.dot(nt(chosen, rows, HI), rows, precision=HI, preferred_element_type=F32)
        band = part if band is None else band + part
    cross_ref[...] = total
    band_ref[...] = band


def cross_and_band(place, mine, other, start, second):
    vmem = pl.BlockSpec(memory_space=pltpu.VMEM)
    return pl.pallas_call(
        cross_kernel,
        out_shape=(
            jax.ShapeDtypeStruct((mine.shape[1], 512), F32),
            jax.ShapeDtypeStruct((16, 512), F32),
        ),
        in_specs=[pl.BlockSpec(memory_space=pltpu.SMEM)] + [vmem] * 4,
        out_specs=(vmem, vmem),
        compiler_params=pltpu.CompilerParams(vmem_limit_bytes=16 * 2**20),
        cost_estimate=pl.CostEstimate(flops=10**9, bytes_accessed=4 * 2**20, transcendentals=0),
        name="cross_and_band",
    )(place, mine, other, start, second)


def half_columns(place):
    return pl.ds(pl.multiple_of(place * 896, 128), 896)


def feedback_kernel(
    core_ref, rows_ref, other_ref, start_ref, inverse_ref, blend_ref, out_ref, basis_ref
):
    basis = nt(start_ref[...], inverse_ref[...], HI).astype(BF16)
    basis_ref[...] = basis
    for place, project_ref in ((core_ref[0], rows_ref), (1 - core_ref[0], other_ref)):
        at = half_columns(place)
        product = nt(basis, project_ref[...])
        out_ref[:, at] = (blend_ref[:, at].astype(F32) - 0.4 * product).astype(BF16)


def update_kernel(
    at_ref, squares_ref, rows_ref, other_ref, basis_ref, weight_ref, out_ref, factor_ref
):
    basis = basis_ref[...]
    squares = jnp.sum(squares_ref[...], axis=0, keepdims=True)
    rms = jnp.sqrt(squares / DF + 1e-06)
    rank = lax.broadcasted_iota(jnp.int32, (16, 512), 1)
    row = lax.broadcasted_iota(jnp.int32, (16, 512), 0)
    chosen = (rank == row + at_ref[1]).astype(BF16)
    for place, project_ref in ((at_ref[0], rows_ref), (1 - at_ref[0], other_ref)):
        at = half_columns(place)
        factor = (project_ref[...].astype(F32) / rms).astype(BF16)
        product = nt(basis, factor)
        step = 2.0 * math.sqrt(DM / DF) * product
        out_ref[:, at] = (weight_ref[:, at].astype(F32) - step).astype(BF16)
        factor_ref[:, at] = nt(chosen, factor).astype(BF16)


def tail_call(kernel, name, flops, outs, *operands):
    vmem = pl.BlockSpec(memory_space=pltpu.VMEM)
    return pl.pallas_call(
        kernel,
        out_shape=tuple(jax.ShapeDtypeStruct(shape, BF16) for shape in outs),
        in_specs=[pl.BlockSpec(memory_space=pltpu.SMEM)] + [vmem] * (len(operands) - 1),
        out_specs=(vmem,) * len(outs),
        compiler_params=pltpu.CompilerParams(vmem_limit_bytes=16 * 2**20),
        cost_estimate=pl.CostEstimate(flops=flops, bytes_accessed=4 * 2**20, transcendentals=0),
        name=name,
    )(*operands)


def local(momentum, gradient, weight, right_factor):
    fsdp, tp = lax.axis_index("fsdp"), lax.axis_index("tp")
    group = (fsdp + fsdp // 2) % 2

    blend = (momentum.astype(F32) + gradient.astype(F32)).astype(BF16)

    half = blend.shape[1] // 2
    columns = lambda place: lax.dynamic_slice_in_dim(blend, place * half, half, axis=1)
    mine, other = columns(group), from_core(columns(1 - group))

    rows = lax.all_gather(right_factor, "fsdp", axis_index_groups=DEEP)
    others = from_core(rows)
    first = (jnp.arange(Z) + group)[:, None, None] % 2 == 0
    factor = jnp.stack([jnp.where(first, rows, others), jnp.where(first, others, rows)], axis=1)
    factor = factor.reshape(512, -1)
    partial = nt(blend, factor)
    pieces = lax.all_to_all(partial.reshape(16, 16, 512), "tp", 0, 0)
    start = spread(jnp.sum(pieces, axis=0), "tp", None, 16).reshape(256, 512)
    start, other = lax.optimization_barrier((start, other))
    second = from_core(start)

    place = (16 * (2 * tp + group)).astype(jnp.int32).reshape(1)
    cross, band = cross_and_band(place, mine, other, start, second)
    cross = lax.psum_scatter(
        cross.reshape(16, 56, 512), "fsdp", scatter_dimension=0, axis_index_groups=DEEP
    )
    band = jnp.sum(lax.all_gather(band, "fsdp", axis_index_groups=DEEP), axis=0)
    bands = spread(band, "tp", None, 16)
    gram = by_group(group, bands, from_core(bands), 1).reshape(512, 512)

    inverse = inverse_factor(gram)
    chunk = nt(cross, inverse, HI).astype(BF16)
    rows = lax.all_gather(chunk, "fsdp", axis_index_groups=DEEP).reshape(-1, 512)
    other = from_core(rows)

    total = lambda half: jnp.sum(jnp.square(half.astype(F32)), axis=0)
    squares = jnp.broadcast_to(total(rows) + total(other), (16, 1, 512))
    squares = lax.all_to_all(squares, "tp", 0, 0)
    place = jnp.stack([group, 16 * fsdp]).astype(jnp.int32)
    new_momentum, basis = tail_call(
        feedback_kernel, "feedback", 13 * 10**8, ((256, 1792), (256, 512)),
        place, rows, other, start, inverse, blend,
    )
    squares, new_momentum, basis = lax.optimization_barrier((squares, new_momentum, basis))
    new_weight, new_factor = tail_call(
        update_kernel, "update", 5 * 10**8, ((256, 1792), (16, 1792)),
        place, squares.reshape(16, 512), rows, other, basis, weight,
    )
    return (new_momentum, new_weight, new_factor)


def solution(mesh):
    placed = (P("fsdp", "tp"), P("fsdp", "tp"), P("fsdp", "tp"), P("fsdp", "tp"))
    return jax.shard_map(
        local,
        mesh=mesh,
        in_specs=placed,
        out_specs=(P("fsdp", "tp"), P("fsdp", "tp"), P("fsdp", "tp")),
        check_vma=False,
    )
```
